256 devices in a mesh: tm: 64 (over z, y, x_hi), mp: 4 (over x_lo, core).
Axes of the slice: x: 4 (x_hi: 2, x_lo: 2; x = x_hi * 2 + x_lo), y: 4, z: 8, core: 2. Of those that a mesh axis runs over, the one named last changes fastest.
Arguments:
- frames: bfloat16 [262144, 1024], P('tm', 'mp'), may hold values from -6 to 6
- first_factor: bfloat16 [512, 512, 512], P('tm'), may hold values from -0.25 to 0.25
- second_factor: bfloat16 [512, 512, 512], P('tm'), may hold values from -0.25 to 0.25
- gate_weight: bfloat16 [1024, 1024], P(None, 'mp'), may hold values from -0.1875 to 0.1875
- mix_weight: bfloat16 [1024, 1024], P(None, 'mp'), may hold values from -0.1875 to 0.1875
Outputs:
- mixed: bfloat16 [262144, 1024], P('tm', 'mp')
The draws below stay inside these ranges and needn't reach their ends.
All inputs are finite; a program needn't handle non-finite values.
Results may differ from the reference program's by a relative error of at most 0.0057.
Values may be sent and summed in bfloat16 or wider, within the bound.
A program may use at most 128 MiB of HBM per device.

```python
import jax
import jax.numpy as jnp

NB = 512
D = 1024
FRAMES = 262144


def shard_levels(rng, extent, shards, low, top_value):
    level, own = 1.0, jax.random.fold_in(rng, 6)
    for axis_at, shards_of in shards:
        steps = jnp.exp(jax.random.uniform(jax.random.fold_in(own, axis_at), (shards_of,), jnp.float32, low / len(shards), top_value / len(shards)))
        level = level * jnp.repeat(steps, extent[axis_at] // shards_of).reshape([-1 if axis == axis_at else 1 for axis in range(len(extent))])
    return level


def bell_draw(rng, dims, spread, bound, cuts=(), kind=jnp.bfloat16):
    values = spread * jax.random.normal(rng, dims, jnp.float32)
    if cuts:
        values = values * shard_levels(rng, dims, cuts, -0.22, 0.18)
    return jnp.clip(values, -bound, bound).astype(kind)


def setup_inputs(seed: int = 0) -> dict:
    keys = jax.random.split(jax.random.key(seed), 6)
    frames = bell_draw(keys[0], (FRAMES, D), 1.0, 6.0, ((0, 64), (1, 4)))
    first_factor = bell_draw(keys[1], (NB, NB, NB), NB ** -0.5, 0.25, ((0, 64),))
    second_factor = bell_draw(keys[2], (NB, NB, NB), NB ** -0.5, 0.25, ((0, 64),))
    gate_weight = bell_draw(keys[3], (D, D), D ** -0.5, 0.1875, ((1, 4),))
    mix_weight = bell_draw(keys[4], (D, D), D ** -0.5, 0.1875, ((1, 4),))
    return {"frames": frames, "first_factor": first_factor, "second_factor": second_factor, "gate_weight": gate_weight, "mix_weight": mix_weight}


def reference(frames, first_factor, second_factor, gate_weight, mix_weight):
    gate = jax.nn.sigmoid(jnp.dot(frames, gate_weight, preferred_element_type=jnp.float32))
    grid = frames.reshape(NB, NB, D).astype(jnp.float32)
    first = jnp.einsum("bkj,bjc->bkc", first_factor.astype(jnp.float32), grid)
    gated = (first * gate.reshape(NB, NB, D)).astype(jnp.bfloat16)
    channel = jnp.dot(gated.reshape(NB * NB, D), mix_weight, preferred_element_type=jnp.float32).astype(jnp.bfloat16)
    channel = channel.reshape(NB, NB, D)
    second = jnp.einsum("kmi,ikc->mkc", second_factor.astype(jnp.float32), channel.astype(jnp.float32)).astype(jnp.bfloat16)
    return second.reshape(NB * NB, D)
```

```python
import jax
import jax.numpy as jnp
from jax import lax
from jax.experimental import pallas as pl
from jax.experimental.pallas import tpu as pltpu
from jax.sharding import PartitionSpec as P

MESH = pl.DeviceIdType.MESH
TM, MP = 64, 4
NB, DW = 512, 256
LB = NB // TM
HALF = 128
BF, F32 = jnp.bfloat16, jnp.float32


def partner(tm, u):
    return lax.rem(tm + (u % 8) * 8 + u // 8 % 8, TM)


def kernel(frames, first_factor, second_factor, gate_w, mix_w, out,
           grid, fv, sv, gw, mw, gated, chan, arrived, rows, sums, second,
           local_sem, f_send, f_recv, w_send, w_recv, a_send, a_recv, o_send, o_recv):
    tm, mp = lax.axis_index("tm"), lax.axis_index("mp")

    def columns(q):
        return pl.ds(pl.multiple_of(q * DW, DW), DW)

    def local(src, dst, at):
        return pltpu.make_async_copy(src, dst, local_sem.at[at])

    def remote(src, dst, send, recv, to):
        return pltpu.make_async_remote_copy(
            src_ref=src, dst_ref=dst, send_sem=send, recv_sem=recv, device_id=to, device_id_type=MESH)

    own = [local(frames.at[s * MP + mp], grid.at[s, :, columns(mp)], s) for s in range(2)]
    own += [local(first_factor.at[s * MP + mp], fv.at[s], 2 + s) for s in range(2)]
    own += [local(gate_w, gw.at[mp], 4), local(mix_w, mw.at[mp], 5), local(second_factor, sv, 6)]
    for c in own:
        c.start()

    barrier = pltpu.get_barrier_semaphore()

    def greet(n, _):
        to = lax.rem(tm * MP + mp + n, TM * MP)
        pl.semaphore_signal(barrier, inc=1, device_id=(to // MP, lax.rem(to, MP)), device_id_type=MESH)
        return 0

    lax.fori_loop(1, TM * MP, greet, 0)
    pl.semaphore_wait(barrier, TM * MP - 1)

    def frames_to(s, p):
        to = mp ^ p
        return remote(frames.at[s * MP + to], grid.at[s, :, columns(mp)],
                      f_send.at[s, p - 1], f_recv.at[s, p - 1], (tm, to))

    def weight_moves(w, buf, at):
        far = remote(w, buf.at[mp], w_send.at[at, 0], w_recv.at[at, 0], (tm ^ 1, mp ^ 2))
        near = remote(w, buf.at[mp], w_send.at[at, 1], w_recv.at[at, 1], (tm, mp ^ 1))
        on = remote(buf.at[mp ^ 2], buf.at[mp ^ 2], w_send.at[at, 2], w_recv.at[at, 2], (tm, mp ^ 1))
        return far, near, on

    fr = [[frames_to(s, p) for p in (2, 3, 1)] for s in range(2)]
    gmove, mmove = weight_moves(gate_w, gw, 0), weight_moves(mix_w, mw, 1)
    for c in (fr[0][0], fr[0][1], gmove[0], fr[0][2], gmove[1], mmove[1]):
        c.start()
    gmove[0].wait_recv()
    gmove[2].start()
    gmove[0].wait_send()
    mmove[0].start()
    for c in fr[0]:
        c.wait_send()
    for c in fr[1]:
        c.start()

    def gate_stage(s):
        def part(n, _):
            q, r = n // 2, pl.multiple_of(lax.rem(n, 2) * 256, 256)
            cols = columns(q)
            pre = jnp.dot(grid[s, pl.ds(r, 256), :], gw[q], preferred_element_type=F32)
            mixed = jnp.dot(fv[s, pl.ds(r, 256), :], grid[s, :, cols], preferred_element_type=F32)
            gated[pl.ds(r, 256), cols] = (mixed * jax.nn.sigmoid(pre)).astype(BF)
            return 0

        lax.fori_loop(0, 8, part, 0)

    def mix_stage(s, q):
        def part(n, _):
            r = pl.multiple_of(n * 256, 256)
            y = jnp.dot(gated[pl.ds(r, 256), :], mw[q], preferred_element_type=F32)
            for h in range(2):
                chan[s, q, pl.ds(n * 32, 32), h] = y[:, h * HALF:(h + 1) * HALF].reshape(32, LB, HALF).astype(BF)
            return 0

        lax.fori_loop(0, 2, part, 0)

    def send_whole(q, first):
        def one(u, _):
            to = partner(tm, u)
            remote(chan.at[0, q, to], arrived.at[:, tm, 0, mp], a_send.at[0], a_recv.at[0], (to, q)).start()
            return 0

        lax.fori_loop(first, TM, one, 0)

    def send_half(q, h, first):
        def one(u, _):
            to = partner(tm, u)
            remote(chan.at[1, q, to, h], arrived.at[h, tm, 1, mp], a_send.at[1 + h], a_recv.at[1 + h], (to, q)).start()
            return 0

        lax.fori_loop(first, TM, one, 0)

    for c in fr[0]:
        c.wait_recv()
    gmove[1].wait_recv()
    gmove[2].wait_recv()
    for at in (0, 2, 4):
        own[at].wait()
    gate_stage(0)
    own[5].wait()
    mix_stage(0, mp)
    pltpu.make_async_copy(chan.at[0, mp, tm], arrived.at[:, tm, 0, mp], a_recv.at[0]).start()
    send_whole(mp, 1)
    mmove[1].wait_recv()
    mix_stage(0, mp ^ 1)
    send_whole(mp ^ 1, 0)
    mmove[0].wait_recv()
    mmove[2].start()
    mix_stage(0, mp ^ 2)
    send_whole(mp ^ 2, 0)
    mmove[2].wait_recv()
    mix_stage(0, mp ^ 3)
    send_whole(mp ^ 3, 0)

    for c in fr[1]:
        c.wait_recv()
    for at in (1, 3):
        own[at].wait()
    gate_stage(1)
    for p in range(MP):
        mix_stage(1, mp ^ p)
        if p == 0:
            for h in range(2):
                pltpu.make_async_copy(chan.at[1, mp, tm, h], arrived.at[h, tm, 1, mp], a_recv.at[1 + h]).start()
        send_half(mp ^ p, 0, 1 if p == 0 else 0)
    for p in range(MP):
        send_half(mp ^ p, 1, 1 if p == 0 else 0)

    own[6].wait()
    pltpu.make_async_copy(arrived.at[:, :, 0], arrived.at[:, :, 0], a_recv.at[0]).wait()
    for h in range(2):
        got = arrived.at[h, :, 1]
        pltpu.make_async_copy(got, got, a_recv.at[1 + h]).wait()

        def widen(n, _):
            t = arrived[h, pl.ds(n * 8, 8)]
            rows[pl.ds(pl.multiple_of(n * 512, 512), 512), :] = t.astype(F32).reshape(512, HALF)
            return 0

        lax.fori_loop(0, 8, widen, 0)
        for k in range(LB):
            x = rows[pl.ds(k, NB, stride=LB), :].astype(BF)
            sums[pl.ds(k, NB, stride=LB), :] = jnp.dot(sv[k], x, preferred_element_type=F32)

        def narrow(n, _):
            t = sums[pl.ds(pl.multiple_of(n * 512, 512), 512), :]
            second[h, pl.ds(n * 8, 8)] = t.reshape(8, LB, LB, HALF).astype(BF)
            return 0

        lax.fori_loop(0, 8, narrow, 0)
        half = pl.ds(h * HALF, HALF)
        pltpu.make_async_copy(second.at[h, tm], out.at[:, tm, :, half], o_recv.at[h]).start()

        def place(u, _):
            to = partner(tm, u)
            remote(second.at[h, to], out.at[:, tm, :, half], o_send.at[h], o_recv.at[h], (to, mp)).start()
            return 0

        lax.fori_loop(1, TM, place, 0)

    for c in fr[1]:
        c.wait_send()
    for at in (1, 2):
        gmove[at].wait_send()
    for c in mmove:
        c.wait_send()
    gone = chan.at[0, 0]

    def left(src, sem):
        pltpu.make_async_copy(src, src, sem).wait()

    for p in range(3):
        left(gone, a_send.at[0])
    left(chan.at[0, 0, pl.ds(0, TM - 1)], a_send.at[0])
    for h in range(2):
        for p in range(3):
            left(chan.at[1, 0, :, h], a_send.at[1 + h])
        left(chan.at[1, 0, pl.ds(0, TM - 1), h], a_send.at[1 + h])
        left(second.at[h, pl.ds(0, TM - 1)], o_send.at[h])
        half = pl.ds(h * HALF, HALF)
        left(out.at[:, :, :, half], o_recv.at[h])


def on_device(frames, first_factor, second_factor, gate_w, mix_w):
    frames = frames.reshape(LB, NB, DW)
    out = pl.pallas_call(
        kernel,
        out_shape=jax.ShapeDtypeStruct((LB, TM, LB, DW), BF),
        in_specs=[pl.BlockSpec(memory_space=pl.ANY)] * 5,
        out_specs=pl.BlockSpec(memory_space=pl.ANY),
        scratch_shapes=[
            pltpu.VMEM((2, NB, MP * DW), BF),
            pltpu.VMEM((2, NB, NB), BF),
            pltpu.VMEM((LB, NB, NB), BF),
            pltpu.VMEM((MP, MP * DW, DW), BF),
            pltpu.VMEM((MP, MP * DW, DW), BF),
            pltpu.VMEM((NB, MP * DW), BF),
            pltpu.VMEM((2, MP, TM, 2, LB, HALF), BF),
            pltpu.VMEM((2, TM, 2, MP, LB, HALF), BF),
            pltpu.VMEM((NB * LB, HALF), F32),
            pltpu.VMEM((NB * LB, HALF), F32),
            pltpu.VMEM((2, TM, LB, LB, HALF), BF),
            pltpu.SemaphoreType.DMA((7,)),
            pltpu.SemaphoreType.DMA((2, 3)),
            pltpu.SemaphoreType.DMA((2, 3)),
            pltpu.SemaphoreType.DMA((2, 3)),
            pltpu.SemaphoreType.DMA((2, 3)),
            pltpu.SemaphoreType.DMA((3,)),
            pltpu.SemaphoreType.DMA((3,)),
            pltpu.SemaphoreType.DMA((2,)),
            pltpu.SemaphoreType.DMA((2,)),
        ],
        compiler_params=pltpu.CompilerParams(
            collective_id=0, has_side_effects=True, vmem_limit_bytes=48 << 20),
        cost_estimate=pl.CostEstimate(flops=6_500_000_000, bytes_accessed=16 << 20, transcendentals=1 << 20),
        name="monarch",
    )(frames, first_factor, second_factor, gate_w, mix_w)
    return out.reshape(LB * NB, DW)


def solution(mesh):
    in_specs = (
        P("tm", "mp"),
        P("tm", None, None),
        P("tm", None, None),
        P(None, "mp"),
        P(None, "mp"),
    )
    return jax.shard_map(
        on_device, mesh=mesh, in_specs=in_specs, out_specs=P("tm", "mp"), check_vma=False
    )
```

```python
import jax
import jax.numpy as jnp
from jax import lax
from jax.experimental import pallas as pl
from jax.experimental.pallas import tpu as pltpu
from jax.sharding import PartitionSpec as P

MESH = pl.DeviceIdType.MESH
TM, MP = 64, 4
NB, DW = 512, 256
LB = NB // TM
HALF = 128
BF, F32 = jnp.bfloat16, jnp.float32


def partner(tm, u):
    return lax.rem(tm + (u % 8) * 8 + u // 8 % 8, TM)


def kernel(frames, first_factor, second_factor, gate_w, mix_w, out,
           grid, fv, sv, gw, mw, gated, chan, arrived, rows, sums, second,
           local_sem, f_send, f_recv, w_send, w_recv, a_send, a_recv, o_send, o_recv, in_sem):
    tm, mp = lax.axis_index("tm"), lax.axis_index("mp")

    def columns(q):
        return pl.ds(pl.multiple_of(q * DW, DW), DW)

    def local(src, dst, at):
        return pltpu.make_async_copy(src, dst, local_sem.at[at])

    def remote(src, dst, send, recv, to):
        return pltpu.make_async_remote_copy(
            src_ref=src, dst_ref=dst, send_sem=send, recv_sem=recv, device_id=to, device_id_type=MESH)

    own = [local(frames.at[s * MP + mp], grid.at[s, :, columns(mp)], s) for s in range(2)]
    own += [local(first_factor.at[s * MP + mp], fv.at[s], 2 + s) for s in range(2)]
    own += [local(gate_w, gw.at[mp], 4), local(mix_w, mw.at[mp], 5), local(second_factor, sv, 6)]
    for c in own:
        c.start()

    z, y, x = tm // 8, tm // 2 % 4, lax.rem(tm, 2) * MP + mp

    def along_x(sem):
        for n in range(1, 8):
            to = x ^ n
            pl.semaphore_signal(sem, inc=1, device_id=(tm // 2 * 2 + to // MP, lax.rem(to, MP)), device_id_type=MESH)

    def along_y(sem):
        for n in range(1, 4):
            to = z * 8 + lax.rem(y + n, 4) * 2 + lax.rem(tm, 2)
            pl.semaphore_signal(sem, inc=1, device_id=(to, mp), device_id_type=MESH)

    def along_z(sem):
        for n in range(1, 8):
            pl.semaphore_signal(sem, inc=1, device_id=(lax.rem(tm + n * 8, TM), mp), device_id_type=MESH)

    barrier = pltpu.get_barrier_semaphore()
    along_x(barrier)
    along_y(barrier)
    along_z(barrier)
    pl.semaphore_wait(barrier, 17)

    def frames_to(s, p):
        to = mp ^ p
        return remote(frames.at[s * MP + to], grid.at[s, :, columns(mp)],
                      f_send.at[s, p - 1], f_recv.at[s, p - 1], (tm, to))

    def weight_moves(w, buf, at):
        far = remote(w, buf.at[mp], w_send.at[at, 0], w_recv.at[at, 0], (tm ^ 1, mp ^ 2))
        near = remote(w, buf.at[mp], w_send.at[at, 1], w_recv.at[at, 1], (tm, mp ^ 1))
        on = remote(buf.at[mp ^ 2], buf.at[mp ^ 2], w_send.at[at, 2], w_recv.at[at, 2], (tm, mp ^ 1))
        return far, near, on

    fr = [[frames_to(s, p) for p in (2, 3, 1)] for s in range(2)]
    gmove, mmove = weight_moves(gate_w, gw, 0), weight_moves(mix_w, mw, 1)
    for c in (fr[0][0], fr[0][1], gmove[0], fr[0][2], gmove[1], mmove[1]):
        c.start()
    along_y(in_sem.at[0])
    pl.semaphore_wait(in_sem.at[0], 3)
    along_z(in_sem.at[1])
    pl.semaphore_wait(in_sem.at[1], 7)
    gmove[0].wait_recv()
    gmove[2].start()
    gmove[0].wait_send()
    mmove[0].start()
    for c in fr[0]:
        c.wait_send()
    for c in fr[1]:
        c.start()

    def gate_stage(s):
        def part(n, _):
            q, r = n // 2, pl.multiple_of(lax.rem(n, 2) * 256, 256)
            cols = columns(q)
            pre = jnp.dot(grid[s, pl.ds(r, 256), :], gw[q], preferred_element_type=F32)
            mixed = jnp.dot(fv[s, pl.ds(r, 256), :], grid[s, :, cols], preferred_element_type=F32)
            gated[pl.ds(r, 256), cols] = (mixed * jax.nn.sigmoid(pre)).astype(BF)
            return 0

        lax.fori_loop(0, 8, part, 0)

    def mix_stage(s, q):
        def part(n, _):
            r = pl.multiple_of(n * 256, 256)
            y = jnp.dot(gated[pl.ds(r, 256), :], mw[q], preferred_element_type=F32)
            for h in range(2):
                chan[s, q, pl.ds(n * 32, 32), h] = y[:, h * HALF:(h + 1) * HALF].reshape(32, LB, HALF).astype(BF)
            return 0

        lax.fori_loop(0, 2, part, 0)

    def send_whole(q, first):
        def one(u, _):
            to = partner(tm, u)
            remote(chan.at[0, q, to], arrived.at[:, tm, 0, mp], a_send.at[0], a_recv.at[0], (to, q)).start()
            return 0

        lax.fori_loop(first, TM, one, 0)

    def send_half(q, h, first):
        def one(u, _):
            to = partner(tm, u)
            remote(chan.at[1, q, to, h], arrived.at[h, tm, 1, mp], a_send.at[1 + h], a_recv.at[1 + h], (to, q)).start()
            return 0

        lax.fori_loop(first, TM, one, 0)

    for c in fr[0]:
        c.wait_recv()
    gmove[1].wait_recv()
    gmove[2].wait_recv()
    for at in (0, 2, 4):
        own[at].wait()
    gate_stage(0)
    own[5].wait()
    mix_stage(0, mp)
    pltpu.make_async_copy(chan.at[0, mp, tm], arrived.at[:, tm, 0, mp], a_recv.at[0]).start()
    send_whole(mp, 1)
    mmove[1].wait_recv()
    mix_stage(0, mp ^ 1)
    send_whole(mp ^ 1, 0)
    mmove[0].wait_recv()
    mmove[2].start()
    mix_stage(0, mp ^ 2)
    send_whole(mp ^ 2, 0)
    mmove[2].wait_recv()
    mix_stage(0, mp ^ 3)
    send_whole(mp ^ 3, 0)

    for c in fr[1]:
        c.wait_recv()
    for at in (1, 3):
        own[at].wait()
    gate_stage(1)
    for p in range(MP):
        mix_stage(1, mp ^ p)
        if p == 0:
            for h in range(2):
                pltpu.make_async_copy(chan.at[1, mp, tm, h], arrived.at[h, tm, 1, mp], a_recv.at[1 + h]).start()
        send_half(mp ^ p, 0, 1 if p == 0 else 0)
    for p in range(MP):
        send_half(mp ^ p, 1, 1 if p == 0 else 0)

    own[6].wait()
    pltpu.make_async_copy(arrived.at[:, :, 0], arrived.at[:, :, 0], a_recv.at[0]).wait()
    for h in range(2):
        got = arrived.at[h, :, 1]
        pltpu.make_async_copy(got, got, a_recv.at[1 + h]).wait()

        def widen(n, _):
            t = arrived[h, pl.ds(n * 8, 8)]
            rows[pl.ds(pl.multiple_of(n * 512, 512), 512), :] = t.astype(F32).reshape(512, HALF)
            return 0

        lax.fori_loop(0, 8, widen, 0)
        for k in range(LB):
            x = rows[pl.ds(k, NB, stride=LB), :].astype(BF)
            sums[pl.ds(k, NB, stride=LB), :] = jnp.dot(sv[k], x, preferred_element_type=F32)

        def narrow(n, _):
            t = sums[pl.ds(pl.multiple_of(n * 512, 512), 512), :]
            second[h, pl.ds(n * 8, 8)] = t.reshape(8, LB, LB, HALF).astype(BF)
            return 0

        lax.fori_loop(0, 8, narrow, 0)
        half = pl.ds(h * HALF, HALF)
        pltpu.make_async_copy(second.at[h, tm], out.at[:, tm, :, half], o_recv.at[h]).start()

        def place(u, _):
            to = partner(tm, u)
            remote(second.at[h, to], out.at[:, tm, :, half], o_send.at[h], o_recv.at[h], (to, mp)).start()
            return 0

        lax.fori_loop(1, TM, place, 0)

    for c in fr[1]:
        c.wait_send()
    for at in (1, 2):
        gmove[at].wait_send()
    for c in mmove:
        c.wait_send()
    gone = chan.at[0, 0]

    def left(src, sem):
        pltpu.make_async_copy(src, src, sem).wait()

    for p in range(3):
        left(gone, a_send.at[0])
    left(chan.at[0, 0, pl.ds(0, TM - 1)], a_send.at[0])
    for h in range(2):
        for p in range(3):
            left(chan.at[1, 0, :, h], a_send.at[1 + h])
        left(chan.at[1, 0, pl.ds(0, TM - 1), h], a_send.at[1 + h])
        left(second.at[h, pl.ds(0, TM - 1)], o_send.at[h])
        half = pl.ds(h * HALF, HALF)
        left(out.at[:, :, :, half], o_recv.at[h])


def on_device(frames, first_factor, second_factor, gate_w, mix_w):
    frames = frames.reshape(LB, NB, DW)
    out = pl.pallas_call(
        kernel,
        out_shape=pltpu.VMEM((LB, TM, LB, DW), BF),
        in_specs=[pl.BlockSpec(memory_space=pltpu.HBM)] * 5,
        out_specs=pl.BlockSpec(memory_space=pl.ANY),
        scratch_shapes=[
            pltpu.VMEM((2, NB, MP * DW), BF),
            pltpu.VMEM((2, NB, NB), BF),
            pltpu.VMEM((LB, NB, NB), BF),
            pltpu.VMEM((MP, MP * DW, DW), BF),
            pltpu.VMEM((MP, MP * DW, DW), BF),
            pltpu.VMEM((NB, MP * DW), BF),
            pltpu.VMEM((2, MP, TM, 2, LB, HALF), BF),
            pltpu.VMEM((2, TM, 2, MP, LB, HALF), BF),
            pltpu.VMEM((NB * LB, HALF), F32),
            pltpu.VMEM((NB * LB, HALF), F32),
            pltpu.VMEM((2, TM, LB, LB, HALF), BF),
            pltpu.SemaphoreType.DMA((7,)),
            pltpu.SemaphoreType.DMA((2, 3)),
            pltpu.SemaphoreType.DMA((2, 3)),
            pltpu.SemaphoreType.DMA((2, 3)),
            pltpu.SemaphoreType.DMA((2, 3)),
            pltpu.SemaphoreType.DMA((3,)),
            pltpu.SemaphoreType.DMA((3,)),
            pltpu.SemaphoreType.DMA((2,)),
            pltpu.SemaphoreType.DMA((2,)),
            pltpu.SemaphoreType.REGULAR((2,)),
        ],
        compiler_params=pltpu.CompilerParams(
            collective_id=0, has_side_effects=True, vmem_limit_bytes=56 << 20),
        cost_estimate=pl.CostEstimate(flops=6_500_000_000, bytes_accessed=16 << 20, transcendentals=1 << 20),
        name="monarch",
    )(frames, first_factor, second_factor, gate_w, mix_w)
    return out.reshape(LB * NB, DW)


def solution(mesh):
    in_specs = (
        P("tm", "mp"),
        P("tm", None, None),
        P("tm", None, None),
        P(None, "mp"),
        P(None, "mp"),
    )
    return jax.shard_map(
        on_device, mesh=mesh, in_specs=in_specs, out_specs=P("tm", "mp"), check_vma=False
    )
```

```python
import jax
import jax.numpy as jnp
from jax import lax
from jax.experimental import pallas as pl
from jax.experimental.pallas import tpu as pltpu
from jax.sharding import PartitionSpec as P

MESH = pl.DeviceIdType.MESH
TM, MP = 64, 4
NB, DW = 512, 256
LB = NB // TM
HALF = 128
ST = 4
KH, TH = NB // 2, TM // 2
QR = 160
BF, F32 = jnp.bfloat16, jnp.float32


def partner(tm, u):
    return lax.rem(tm + (u % 8) * 8 + u // 8 % 8, TM)


def partner_half(tm, u):
    return lax.rem(tm // 8 + u % 4, 4) * 8 + lax.rem(tm + u // 4, 8)


def kernel(frames, first_factor, second_factor, gate_w, mix_w, out,
           grid, fv, sv, gw, mw, gated, chan, arrived, rows, sums, second,
           local_sem, f_send, f_recv, w_send, w_recv, a_send, a_recv, o_send, o_recv, in_sem):
    tm, mp = lax.axis_index("tm"), lax.axis_index("mp")
    z, y, x = tm // 8, tm // 2 % 4, lax.rem(tm, 2) * MP + mp
    chip = mp // 2
    half_k = lax.rem(mp + z + jnp.where(z < 4, 1, 0), 2)

    def columns(q):
        return pl.ds(pl.multiple_of(q * DW, DW), DW)

    my_k = pl.ds(pl.multiple_of(half_k * KH, KH), KH)

    def local(src, dst, at):
        return pltpu.make_async_copy(src, dst, local_sem.at[at])

    def remote(src, dst, send, recv, to):
        return pltpu.make_async_remote_copy(
            src_ref=src, dst_ref=dst, send_sem=send, recv_sem=recv, device_id=to, device_id_type=MESH)

    own = [local(frames.at[2 * s + chip], grid.at[s, :, columns(mp)], s) for s in range(ST)]
    own += [local(first_factor.at[2 * s + chip, my_k], fv.at[s], ST + s) for s in range(ST)]
    own += [local(gate_w, gw.at[mp], 2 * ST), local(mix_w, mw.at[mp], 2 * ST + 1), local(second_factor, sv, 2 * ST + 2)]
    for c in own:
        c.start()

    def along_x(sem):
        for n in range(1, 8):
            to = x ^ n
            pl.semaphore_signal(sem, inc=1, device_id=(tm // 2 * 2 + to // MP, lax.rem(to, MP)), device_id_type=MESH)

    def along_y(sem):
        for n in range(1, 4):
            to = z * 8 + lax.rem(y + n, 4) * 2 + lax.rem(tm, 2)
            pl.semaphore_signal(sem, inc=1, device_id=(to, mp), device_id_type=MESH)

    def along_z(sem):
        for n in range(1, 8):
            pl.semaphore_signal(sem, inc=1, device_id=(lax.rem(tm + n * 8, TM), mp), device_id_type=MESH)

    barrier = pltpu.get_barrier_semaphore()
    along_x(barrier)
    along_y(barrier)
    along_z(barrier)
    pl.semaphore_wait(barrier, 17)

    other = (tm, mp ^ 1)

    def frame_moves(s):
        cross = remote(frames.at[2 * s + 1 - chip], grid.at[s, :, columns(mp)], f_send.at[s, 0], f_recv.at[s, 0], (tm, mp ^ 2))
        near = remote(frames.at[2 * s + chip], grid.at[s, :, columns(mp)], f_send.at[s, 1], f_recv.at[s, 1], other)
        came = grid.at[s, :, columns(mp ^ 2)]
        return cross, near, remote(came, came, f_send.at[s, 2], f_recv.at[s, 2], other)

    def weight_moves(w, buf, at):
        def move(src, slot, part, kind, to):
            return remote(src.at[part], buf.at[slot, part], w_send.at[at, kind], w_recv.at[at, kind], to)

        def quarter(n):
            return pl.ds(pl.multiple_of(lax.rem(y + 4 - n, 4) * QR, 16), QR)

        held, rest, far = mp ^ 2, pl.ds(4 * QR, MP * DW - 4 * QR), (tm ^ 1, mp ^ 2)
        first, last = move(w, mp, quarter(0), 0, far), move(w, mp, rest, 1, far)
        near = remote(w, buf.at[mp], w_send.at[at, 2], w_recv.at[at, 2], other)
        line = [move(buf.at[held], held, quarter(0), 2 + n,
                     (z * 8 + lax.rem(y + n, 4) * 2 + lax.rem(tm, 2), mp)) for n in range(1, 4)]
        on = [move(buf.at[held], held, quarter(n), 6 + n, other) for n in range(4)]
        on.append(move(buf.at[held], held, rest, 10, other))
        return first, last, near, line, on

    fr = [frame_moves(s) for s in range(ST)]
    gmoves, mmoves = weight_moves(gate_w, gw, 0), weight_moves(mix_w, mw, 1)
    gfirst, glast, gnear, gline, gon = gmoves
    mfirst, mlast, mnear, mline, mon = mmoves
    for c in (gfirst, fr[0][0], fr[0][1], gnear, mnear):
        c.start()
    along_y(in_sem.at[0])
    pl.semaphore_wait(in_sem.at[0], 3)
    along_z(in_sem.at[1])
    gfirst.wait_recv()
    for c in (*gline, gon[0]):
        c.start()
    gfirst.wait_send()
    glast.start()
    pl.semaphore_wait(in_sem.at[1], 7)

    def gate_part(s, q):
        cols = columns(q)
        pre = jnp.dot(grid[s, my_k, :], gw[q], preferred_element_type=F32)
        mixed = jnp.dot(fv[s], grid[s, :, cols], preferred_element_type=F32)
        gated[s, :, cols] = (mixed * jax.nn.sigmoid(pre)).astype(BF)

    def gate_parts(s, first, last):
        def part(p, _):
            gate_part(s, mp ^ p)
            return 0

        lax.fori_loop(first, last, part, 0)

    def send_whole(s, q, may_be_own):
        def one(u, _):
            to = half_k * TH + partner_half(tm, u)
            src, dst = chan.at[s, q, lax.rem(to, TH)], arrived.at[:, tm, 2 * s + chip]

            def away():
                remote(src, dst, a_send.at[0], a_recv.at[0], (to, q)).start()

            if may_be_own:
                pl.when(to != tm)(away)
                pl.when(to == tm)(lambda: pltpu.make_async_copy(src, dst, a_recv.at[0]).start())
            else:
                away()
            return 0

        lax.fori_loop(0, TH, one, 0, unroll=4)

    def send_half(s, q, h, may_be_own):
        def one(u, _):
            to = half_k * TH + partner_half(tm, u)
            src, dst = chan.at[s, q, lax.rem(to, TH), h], arrived.at[h, tm, 2 * s + chip]

            def away():
                remote(src, dst, a_send.at[1 + h], a_recv.at[1 + h], (to, q)).start()

            if may_be_own:
                pl.when(to != tm)(away)
                pl.when(to == tm)(lambda: pltpu.make_async_copy(src, dst, a_recv.at[1 + h]).start())
            else:
                away()
            return 0

        lax.fori_loop(0, TH, one, 0, unroll=4)

    def mix(s, q):
        v = jnp.dot(gated[s], mw[q], preferred_element_type=F32)
        for h in range(2):
            chan[s, q, :, h] = v[:, h * HALF:(h + 1) * HALF].reshape(TH, LB, HALF).astype(BF)

    def mix_and_send(s, first, last):
        if first == 0:
            mix(s, mp)
            send_whole(s, mp, True)
        def part(p, _):
            mix(s, mp ^ p)
            send_whole(s, mp ^ p, False)
            return 0

        lax.fori_loop(max(first, 1), last, part, 0)

    def mix_and_send_half(s):
        mix(s, mp)
        send_half(s, mp, 0, True)

        def part(p, _):
            mix(s, mp ^ p)
            send_half(s, mp ^ p, 0, False)
            return 0

        lax.fori_loop(1, MP, part, 0)

    def send_other_half(s):
        send_half(s, mp, 1, True)

        def part(p, _):
            send_half(s, mp ^ p, 1, False)
            return 0

        lax.fori_loop(1, MP, part, 0)

    def take(s):
        fr[s][0].wait_recv()
        fr[s][2].start()
        if s + 1 < ST:
            fr[s][0].wait_send()
            fr[s + 1][0].start()
            fr[s + 1][1].start()

    def whole(s):
        own[s].wait()
        own[ST + s].wait()
        fr[s][1].wait_recv()
        fr[s][2].wait_recv()

    def gather(last, line, on):
        for n in range(3):
            line[n].wait_recv()
            on[n + 1].start()
        last.wait_recv()
        on[4].start()

    take(0)
    gather(glast, gline, gon)
    glast.wait_send()
    mfirst.start()
    whole(0)
    own[2 * ST].wait()
    gnear.wait_recv()
    gate_parts(0, 0, 2)
    for c in gon:
        c.wait_recv()
    gate_parts(0, 2, MP)
    mfirst.wait_recv()
    for c in (*mline, mon[0]):
        c.start()
    mfirst.wait_send()
    mlast.start()
    own[2 * ST + 1].wait()
    mnear.wait_recv()
    mix_and_send(0, 0, 2)
    take(1)
    whole(1)
    gate_parts(1, 0, MP)
    mix_and_send(1, 0, 2)
    gather(mlast, mline, mon)
    for c in mon:
        c.wait_recv()
    mix_and_send(0, 2, MP)
    mix_and_send(1, 2, MP)
    for s in (2, 3):
        take(s)
        whole(s)
        gate_parts(s, 0, MP)
        mix_and_send_half(s)
    for s in (2, 3):
        send_other_half(s)

    own[2 * ST + 2].wait()
    got = arrived.at[:, :, pl.ds(0, 4)]
    pltpu.make_async_copy(got, got, a_recv.at[0]).wait()
    for h in range(2):
        got = arrived.at[h, :, pl.ds(4, 4)]
        pltpu.make_async_copy(got, got, a_recv.at[1 + h]).wait()

        def widen(n, _):
            t = arrived[h, pl.ds(n * 8, 8)]
            rows[pl.ds(pl.multiple_of(n * 512, 512), 512), :] = t.astype(F32).reshape(512, HALF)
            return 0

        lax.fori_loop(0, 8, widen, 0)
        for k in range(LB):
            v = rows[pl.ds(k, NB, stride=LB), :].astype(BF)
            sums[pl.ds(k, NB, stride=LB), :] = jnp.dot(sv[k], v, preferred_element_type=F32)

        def narrow(n, _):
            t = sums[pl.ds(pl.multiple_of(n * 512, 512), 512), :]
            second[h, pl.ds(n * 8, 8)] = t.reshape(8, LB, LB, HALF).astype(BF)
            return 0

        lax.fori_loop(0, 8, narrow, 0)
        half = pl.ds(h * HALF, HALF)
        pltpu.make_async_copy(second.at[h, tm], out.at[:, tm, :, half], o_recv.at[h]).start()

        def place(u, _):
            to = partner(tm, u)
            remote(second.at[h, to], out.at[:, tm, :, half], o_send.at[h], o_recv.at[h], (to, mp)).start()
            return 0

        lax.fori_loop(1, TM, place, 0, unroll=3)

    for s in range(ST):
        fr[s][1].wait_send()
        fr[s][2].wait_send()
    fr[ST - 1][0].wait_send()
    for c in (gnear, *gline, *gon, mnear, mlast, *mline, *mon):
        c.wait_send()

    def left(src, sem):
        pltpu.make_async_copy(src, src, sem).wait()

    keeps = tm // TH == half_k

    def drop_own(part, sem):
        whole, rest = part(TH), part(TH - 1)
        pl.when(keeps)(lambda: left(rest, sem))
        pl.when(jnp.logical_not(keeps))(lambda: left(whole, sem))

    for s in (0, 1):
        for q in range(1, MP):
            left(chan.at[s, q], a_send.at[0])
        drop_own(lambda n: chan.at[s, 0, pl.ds(0, n)], a_send.at[0])
    for h in range(2):
        for s in (2, 3):
            for q in range(1, MP):
                left(chan.at[s, q, :, h], a_send.at[1 + h])
            drop_own(lambda n: chan.at[s, 0, pl.ds(0, n), h], a_send.at[1 + h])
        left(second.at[h, pl.ds(0, TM - 1)], o_send.at[h])
        half = pl.ds(h * HALF, HALF)
        left(out.at[:, :, :, half], o_recv.at[h])


def on_device(frames, first_factor, second_factor, gate_w, mix_w):
    frames = frames.reshape(LB, NB, DW)
    out = pl.pallas_call(
        kernel,
        out_shape=pltpu.VMEM((LB, TM, LB, DW), BF),
        in_specs=[pl.BlockSpec(memory_space=pltpu.HBM)] * 5,
        out_specs=pl.BlockSpec(memory_space=pl.ANY),
        scratch_shapes=[
            pltpu.VMEM((ST, NB, MP * DW), BF),
            pltpu.VMEM((ST, KH, NB), BF),
            pltpu.VMEM((LB, NB, NB), BF),
            pltpu.VMEM((MP, MP * DW, DW), BF),
            pltpu.VMEM((MP, MP * DW, DW), BF),
            pltpu.VMEM((ST, KH, MP * DW), BF),
            pltpu.VMEM((ST, MP, TH, 2, LB, HALF), BF),
            pltpu.VMEM((2, TM, LB, LB, HALF), BF),
            pltpu.VMEM((NB * LB, HALF), F32),
            pltpu.VMEM((NB * LB, HALF), F32),
            pltpu.VMEM((2, TM, LB, LB, HALF), BF),
            pltpu.SemaphoreType.DMA((2 * ST + 3,)),
            pltpu.SemaphoreType.DMA((ST, 3)),
            pltpu.SemaphoreType.DMA((ST, 3)),
            pltpu.SemaphoreType.DMA((2, 11)),
            pltpu.SemaphoreType.DMA((2, 11)),
            pltpu.SemaphoreType.DMA((3,)),
            pltpu.SemaphoreType.DMA((3,)),
            pltpu.SemaphoreType.DMA((2,)),
            pltpu.SemaphoreType.DMA((2,)),
            pltpu.SemaphoreType.REGULAR((2,)),
        ],
        compiler_params=pltpu.CompilerParams(
            collective_id=0, has_side_effects=True, vmem_limit_bytes=56 << 20),
        cost_estimate=pl.CostEstimate(flops=6_500_000_000, bytes_accessed=16 << 20, transcendentals=1 << 20),
        name="monarch",
    )(frames, first_factor, second_factor, gate_w, mix_w)
    return out.reshape(LB * NB, DW)


def solution(mesh):
    in_specs = (
        P("tm", "mp"),
        P("tm", None, None),
        P("tm", None, None),
        P(None, "mp"),
        P(None, "mp"),
    )
    return jax.shard_map(
        on_device, mesh=mesh, in_specs=in_specs, out_specs=P("tm", "mp"), check_vma=False
    )
```

```python
import jax
import jax.numpy as jnp
from jax import lax
from jax.experimental import pallas as pl
from jax.experimental.pallas import tpu as pltpu
from jax.sharding import PartitionSpec as P

MESH = pl.DeviceIdType.MESH
TM, MP = 64, 4
NB, DW = 512, 256
LB = NB // TM
HALF = 128
ST = 4
KH, TH = NB // 2, TM // 2
QR = 160
BF, F32 = jnp.bfloat16, jnp.float32


def partner(tm, u):
    return lax.rem(tm + (u % 8) * 8 + u // 8 % 8, TM)


def partner_half(tm, u):
    return lax.rem(tm // 8 + u % 4, 4) * 8 + lax.rem(tm + u // 4, 8)


def kernel(frames, first_factor, second_factor, gate_w, mix_w, out,
           grid, fv, sv, gw, mw, gated, chan, arrived, rows, sums, second,
           local_sem, f_send, f_recv, w_send, w_recv, a_send, a_recv, o_send, o_recv, in_sem):
    tm, mp = lax.axis_index("tm"), lax.axis_index("mp")
    z, y, x = tm // 8, tm // 2 % 4, lax.rem(tm, 2) * MP + mp
    chip = mp // 2
    half_k = lax.rem(mp + z + jnp.where(z < 4, 1, 0), 2)

    def columns(q):
        return pl.ds(pl.multiple_of(q * DW, DW), DW)

    my_k = pl.ds(pl.multiple_of(half_k * KH, KH), KH)

    def local(src, dst, at):
        return pltpu.make_async_copy(src, dst, local_sem.at[at])

    def remote(src, dst, send, recv, to):
        return pltpu.make_async_remote_copy(
            src_ref=src, dst_ref=dst, send_sem=send, recv_sem=recv, device_id=to, device_id_type=MESH)

    own = [local(frames.at[2 * s + chip], grid.at[s, :, columns(mp)], s) for s in range(ST)]
    own += [local(first_factor.at[2 * s + chip, my_k], fv.at[s], ST + s) for s in range(ST)]
    own += [local(gate_w, gw.at[mp], 2 * ST), local(mix_w, mw.at[mp], 2 * ST + 1), local(second_factor, sv, 2 * ST + 2)]
    for c in own:
        c.start()

    def along_x(sem):
        for n in range(1, 8):
            to = x ^ n
            pl.semaphore_signal(sem, inc=1, device_id=(tm // 2 * 2 + to // MP, lax.rem(to, MP)), device_id_type=MESH)

    def along_y(sem):
        for n in range(1, 4):
            to = z * 8 + lax.rem(y + n, 4) * 2 + lax.rem(tm, 2)
            pl.semaphore_signal(sem, inc=1, device_id=(to, mp), device_id_type=MESH)

    def along_z(sem):
        for n in range(1, 8):
            pl.semaphore_signal(sem, inc=1, device_id=(lax.rem(tm + n * 8, TM), mp), device_id_type=MESH)

    barrier = pltpu.get_barrier_semaphore()
    along_x(barrier)
    along_y(barrier)
    along_z(barrier)
    pl.semaphore_wait(barrier, 17)

    other = (tm, mp ^ 1)

    def frame_moves(s):
        cross = remote(frames.at[2 * s + 1 - chip], grid.at[s, :, columns(mp)], f_send.at[s, 0], f_recv.at[s, 0], (tm, mp ^ 2))
        near = remote(frames.at[2 * s + chip], grid.at[s, :, columns(mp)], f_send.at[s, 1], f_recv.at[s, 1], other)
        came = grid.at[s, :, columns(mp ^ 2)]
        return cross, near, remote(came, came, f_send.at[s, 2], f_recv.at[s, 2], other)

    def weight_moves(w, buf, at):
        def move(src, slot, part, kind, to):
            return remote(src.at[part], buf.at[slot, part], w_send.at[at, kind], w_recv.at[at, kind], to)

        def quarter(n):
            return pl.ds(pl.multiple_of(lax.rem(y + 4 - n, 4) * QR, 16), QR)

        held, rest, far = mp ^ 2, pl.ds(4 * QR, MP * DW - 4 * QR), (tm ^ 1, mp ^ 2)
        first, last = move(w, mp, quarter(0), 0, far), move(w, mp, rest, 1, far)
        near = remote(w, buf.at[mp], w_send.at[at, 2], w_recv.at[at, 2], other)
        line = [move(buf.at[held], held, quarter(0), 2 + n,
                     (z * 8 + lax.rem(y + n, 4) * 2 + lax.rem(tm, 2), mp)) for n in range(1, 4)]
        on = [move(buf.at[held], held, quarter(n), 6 + n, other) for n in range(4)]
        on.append(move(buf.at[held], held, rest, 10, other))
        return first, last, near, line, on

    fr = [frame_moves(s) for s in range(ST)]
    gmoves, mmoves = weight_moves(gate_w, gw, 0), weight_moves(mix_w, mw, 1)
    gfirst, glast, gnear, gline, gon = gmoves
    mfirst, mlast, mnear, mline, mon = mmoves
    for c in (gfirst, fr[0][0], fr[0][1], gnear, mnear):
        c.start()
    along_y(in_sem.at[0])
    pl.semaphore_wait(in_sem.at[0], 3)
    along_z(in_sem.at[1])
    gfirst.wait_recv()
    for c in (*gline, gon[0]):
        c.start()
    gfirst.wait_send()
    glast.start()
    pl.semaphore_wait(in_sem.at[1], 7)

    def gate_part(s, q):
        cols = columns(q)
        pre = jnp.dot(grid[s, my_k, :], gw[q], preferred_element_type=F32)
        mixed = jnp.dot(fv[s], grid[s, :, cols], preferred_element_type=F32)
        gated[s, :, cols] = (mixed * jax.nn.sigmoid(pre)).astype(BF)

    def gate_parts(s, first, last):
        def part(p, _):
            gate_part(s, mp ^ p)
            return 0

        lax.fori_loop(first, last, part, 0)

    def send_whole(s, q, may_be_own):
        def one(u, _):
            to = half_k * TH + partner_half(tm, u)
            src, dst = chan.at[s, q, lax.rem(to, TH)], arrived.at[:, tm, 2 * s + chip]

            def away():
                remote(src, dst, a_send.at[0], a_recv.at[0], (to, q)).start()

            if may_be_own:
                pl.when(to != tm)(away)
                pl.when(to == tm)(lambda: pltpu.make_async_copy(src, dst, a_recv.at[0]).start())
            else:
                away()
            return 0

        lax.fori_loop(0, TH, one, 0, unroll=4)

    def send_half(s, q, h, may_be_own):
        def one(u, _):
            to = half_k * TH + partner_half(tm, u)
            src, dst = chan.at[s, q, lax.rem(to, TH), h], arrived.at[h, tm, 2 * s + chip]

            def away():
                remote(src, dst, a_send.at[1 + h], a_recv.at[1 + h], (to, q)).start()

            if may_be_own:
                pl.when(to != tm)(away)
                pl.when(to == tm)(lambda: pltpu.make_async_copy(src, dst, a_recv.at[1 + h]).start())
            else:
                away()
            return 0

        lax.fori_loop(0, TH, one, 0, unroll=4)

    def mix(s, q):
        v = jnp.dot(gated[s], mw[q], preferred_element_type=F32)
        for h in range(2):
            chan[s, q, :, h] = v[:, h * HALF:(h + 1) * HALF].reshape(TH, LB, HALF).astype(BF)

    def mix_and_send(s, first, last):
        if first == 0:
            mix(s, mp)
            send_whole(s, mp, True)
        def part(p, _):
            mix(s, mp ^ p)
            send_whole(s, mp ^ p, False)
            return 0

        lax.fori_loop(max(first, 1), last, part, 0)

    def mixes_and_halves(s, first):
        if first == 0:
            mix(s, mp)
            send_half(s, mp, 0, True)

        def part(p, _):
            mix(s, mp ^ p)
            send_half(s, mp ^ p, 0, False)
            return 0

        lax.fori_loop(max(first, 1), MP, part, 0)

    def other_halves(s, first):
        if first == 0:
            send_half(s, mp, 1, True)

        def part(p, _):
            send_half(s, mp ^ p, 1, False)
            return 0

        lax.fori_loop(max(first, 1), MP, part, 0)

    def take(s):
        fr[s][0].wait_recv()
        fr[s][2].start()
        if s + 1 < ST:
            fr[s][0].wait_send()
            fr[s + 1][0].start()
            fr[s + 1][1].start()

    def whole(s):
        own[s].wait()
        own[ST + s].wait()
        fr[s][1].wait_recv()
        fr[s][2].wait_recv()

    def gather(last, line, on):
        for n in range(3):
            line[n].wait_recv()
            on[n + 1].start()
        last.wait_recv()
        on[4].start()

    take(0)
    gather(glast, gline, gon)
    glast.wait_send()
    mfirst.start()
    whole(0)
    own[2 * ST].wait()
    gnear.wait_recv()
    gate_parts(0, 0, 2)
    for c in gon:
        c.wait_recv()
    gate_parts(0, 2, MP)
    mfirst.wait_recv()
    for c in (*mline, mon[0]):
        c.start()
    mfirst.wait_send()
    mlast.start()
    own[2 * ST + 1].wait()
    mnear.wait_recv()
    mix_and_send(0, 0, 2)
    take(1)
    whole(1)
    gate_parts(1, 0, MP)
    mix_and_send(1, 0, 2)
    gather(mlast, mline, mon)
    for c in mon:
        c.wait_recv()
    mix_and_send(0, 2, MP)
    mixes_and_halves(1, 2)
    for s in (2, 3):
        take(s)
        whole(s)
        gate_parts(s, 0, MP)
        mixes_and_halves(s, 0)
        if s == 2:
            other_halves(1, 2)
    for s in (2, 3):
        other_halves(s, 0)

    own[2 * ST + 2].wait()
    got = arrived.at[:, :, pl.ds(0, 3)]
    pltpu.make_async_copy(got, got, a_recv.at[0]).wait()
    for h in range(2):
        got = arrived.at[h, :, pl.ds(3, 5)]
        pltpu.make_async_copy(got, got, a_recv.at[1 + h]).wait()

        def widen(n, _):
            t = arrived[h, pl.ds(n * 8, 8)]
            rows[pl.ds(pl.multiple_of(n * 512, 512), 512), :] = t.astype(F32).reshape(512, HALF)
            return 0

        lax.fori_loop(0, 8, widen, 0)
        for k in range(LB):
            v = rows[pl.ds(k, NB, stride=LB), :].astype(BF)
            sums[pl.ds(k, NB, stride=LB), :] = jnp.dot(sv[k], v, preferred_element_type=F32)

        def narrow(n, _):
            t = sums[pl.ds(pl.multiple_of(n * 512, 512), 512), :]
            second[h, pl.ds(n * 8, 8)] = t.reshape(8, LB, LB, HALF).astype(BF)
            return 0

        lax.fori_loop(0, 8, narrow, 0)
        half = pl.ds(h * HALF, HALF)
        pltpu.make_async_copy(second.at[h, tm], out.at[:, tm, :, half], o_recv.at[h]).start()

        def place(u, _):
            to = partner(tm, u)
            remote(second.at[h, to], out.at[:, tm, :, half], o_send.at[h], o_recv.at[h], (to, mp)).start()
            return 0

        lax.fori_loop(1, TM, place, 0, unroll=3)

    for s in range(ST):
        fr[s][1].wait_send()
        fr[s][2].wait_send()
    fr[ST - 1][0].wait_send()
    for c in (gnear, *gline, *gon, mnear, mlast, *mline, *mon):
        c.wait_send()

    def left(src, sem):
        pltpu.make_async_copy(src, src, sem).wait()

    keeps = tm // TH == half_k

    def drop_own(part, sem):
        whole, rest = part(TH), part(TH - 1)
        pl.when(keeps)(lambda: left(rest, sem))
        pl.when(jnp.logical_not(keeps))(lambda: left(whole, sem))

    for s, whole_columns in ((0, MP), (1, 2)):
        for q in range(1, whole_columns):
            left(chan.at[s, q], a_send.at[0])
        drop_own(lambda n: chan.at[s, 0, pl.ds(0, n)], a_send.at[0])
    for h in range(2):
        for q in range(2, MP):
            left(chan.at[1, q, :, h], a_send.at[1 + h])
        for s in (2, 3):
            for q in range(1, MP):
                left(chan.at[s, q, :, h], a_send.at[1 + h])
            drop_own(lambda n: chan.at[s, 0, pl.ds(0, n), h], a_send.at[1 + h])
        left(second.at[h, pl.ds(0, TM - 1)], o_send.at[h])
        half = pl.ds(h * HALF, HALF)
        left(out.at[:, :, :, half], o_recv.at[h])


def on_device(frames, first_factor, second_factor, gate_w, mix_w):
    frames = frames.reshape(LB, NB, DW)
    out = pl.pallas_call(
        kernel,
        out_shape=pltpu.VMEM((LB, TM, LB, DW), BF),
        in_specs=[pl.BlockSpec(memory_space=pltpu.HBM)] * 5,
        out_specs=pl.BlockSpec(memory_space=pl.ANY),
        scratch_shapes=[
            pltpu.VMEM((ST, NB, MP * DW), BF),
            pltpu.VMEM((ST, KH, NB), BF),
            pltpu.VMEM((LB, NB, NB), BF),
            pltpu.VMEM((MP, MP * DW, DW), BF),
            pltpu.VMEM((MP, MP * DW, DW), BF),
            pltpu.VMEM((ST, KH, MP * DW), BF),
            pltpu.VMEM((ST, MP, TH, 2, LB, HALF), BF),
            pltpu.VMEM((2, TM, LB, LB, HALF), BF),
            pltpu.VMEM((NB * LB, HALF), F32),
            pltpu.VMEM((NB * LB, HALF), F32),
            pltpu.VMEM((2, TM, LB, LB, HALF), BF),
            pltpu.SemaphoreType.DMA((2 * ST + 3,)),
            pltpu.SemaphoreType.DMA((ST, 3)),
            pltpu.SemaphoreType.DMA((ST, 3)),
            pltpu.SemaphoreType.DMA((2, 11)),
            pltpu.SemaphoreType.DMA((2, 11)),
            pltpu.SemaphoreType.DMA((3,)),
            pltpu.SemaphoreType.DMA((3,)),
            pltpu.SemaphoreType.DMA((2,)),
            pltpu.SemaphoreType.DMA((2,)),
            pltpu.SemaphoreType.REGULAR((2,)),
        ],
        compiler_params=pltpu.CompilerParams(
            collective_id=0, has_side_effects=True, vmem_limit_bytes=56 << 20),
        cost_estimate=pl.CostEstimate(flops=6_500_000_000, bytes_accessed=16 << 20, transcendentals=1 << 20),
        name="monarch",
    )(frames, first_factor, second_factor, gate_w, mix_w)
    return out.reshape(LB * NB, DW)


def solution(mesh):
    in_specs = (
        P("tm", "mp"),
        P("tm", None, None),
        P("tm", None, None),
        P(None, "mp"),
        P(None, "mp"),
    )
    return jax.shard_map(
        on_device, mesh=mesh, in_specs=in_specs, out_specs=P("tm", "mp"), check_vma=False
    )
```

```python
import jax
import jax.numpy as jnp
from jax import lax
from jax.experimental import pallas as pl
from jax.experimental.pallas import tpu as pltpu
from jax.sharding import PartitionSpec as P

MESH = pl.DeviceIdType.MESH
TM, MP = 64, 4
NB, DW = 512, 256
LB = NB // TM
HALF = 128
ST = 4
KH, TH = NB // 2, TM // 2
QR = 160
BF, F32 = jnp.bfloat16, jnp.float32


def partner(tm, u):
    return lax.rem(tm + (u % 8) * 8 + u // 8 % 8, TM)


def partner_half(tm, u):
    return lax.rem(tm // 8 + u % 4, 4) * 8 + lax.rem(tm + u // 4, 8)


def kernel(frames, first_factor, second_factor, gate_w, mix_w, out,
           grid, fv, sv, gw, mw, gated, chan, arrived, rows, sums, second,
           local_sem, f_send, f_recv, w_send, w_recv, a_send, a_recv, o_send, o_recv, in_sem):
    tm, mp = lax.axis_index("tm"), lax.axis_index("mp")
    z, y, x = tm // 8, tm // 2 % 4, lax.rem(tm, 2) * MP + mp
    chip = mp // 2
    half_k = lax.rem(mp + z + jnp.where(z < 4, 1, 0), 2)

    def columns(q):
        return pl.ds(pl.multiple_of(q * DW, DW), DW)

    my_k = pl.ds(pl.multiple_of(half_k * KH, KH), KH)

    def local(src, dst, at):
        return pltpu.make_async_copy(src, dst, local_sem.at[at])

    def remote(src, dst, send, recv, to):
        return pltpu.make_async_remote_copy(
            src_ref=src, dst_ref=dst, send_sem=send, recv_sem=recv, device_id=to, device_id_type=MESH)

    own = [local(frames.at[2 * s + chip], grid.at[s, :, columns(mp)], s) for s in range(ST)]
    own += [local(first_factor.at[2 * s + chip, my_k], fv.at[s], ST + s) for s in range(ST)]
    own += [local(gate_w, gw.at[mp], 2 * ST), local(mix_w, mw.at[mp], 2 * ST + 1), local(second_factor, sv, 2 * ST + 2)]
    for c in own:
        c.start()

    def along_x(sem):
        for n in range(1, 8):
            to = x ^ n
            pl.semaphore_signal(sem, inc=1, device_id=(tm // 2 * 2 + to // MP, lax.rem(to, MP)), device_id_type=MESH)

    def along_y(sem):
        for n in range(1, 4):
            to = z * 8 + lax.rem(y + n, 4) * 2 + lax.rem(tm, 2)
            pl.semaphore_signal(sem, inc=1, device_id=(to, mp), device_id_type=MESH)

    def along_z(sem):
        for n in range(1, 8):
            pl.semaphore_signal(sem, inc=1, device_id=(lax.rem(tm + n * 8, TM), mp), device_id_type=MESH)

    barrier = pltpu.get_barrier_semaphore()
    along_x(barrier)
    along_y(barrier)
    along_z(barrier)
    pl.semaphore_wait(barrier, 17)

    other = (tm, mp ^ 1)

    def frame_moves(s):
        cross = remote(frames.at[2 * s + 1 - chip], grid.at[s, :, columns(mp)], f_send.at[s, 0], f_recv.at[s, 0], (tm, mp ^ 2))
        near = remote(frames.at[2 * s + chip], grid.at[s, :, columns(mp)], f_send.at[s, 1], f_recv.at[s, 1], other)
        came = grid.at[s, :, columns(mp ^ 2)]
        return cross, near, remote(came, came, f_send.at[s, 2], f_recv.at[s, 2], other)

    def weight_moves(w, buf, at):
        def move(src, slot, part, kind, to):
            return remote(src.at[part], buf.at[slot, part], w_send.at[at, kind], w_recv.at[at, kind], to)

        def quarter(n):
            return pl.ds(pl.multiple_of(lax.rem(y + 4 - n, 4) * QR, 16), QR)

        held, rest, far = mp ^ 2, pl.ds(4 * QR, MP * DW - 4 * QR), (tm ^ 1, mp ^ 2)
        first, last = move(w, mp, quarter(0), 0, far), move(w, mp, rest, 1, far)
        near = remote(w, buf.at[mp], w_send.at[at, 2], w_recv.at[at, 2], other)
        line = [move(buf.at[held], held, quarter(0), 2 + n,
                     (z * 8 + lax.rem(y + n, 4) * 2 + lax.rem(tm, 2), mp)) for n in range(1, 4)]
        on = [move(buf.at[held], held, quarter(n), 6 + n, other) for n in range(4)]
        on.append(move(buf.at[held], held, rest, 10, other))
        return first, last, near, line, on

    fr = [frame_moves(s) for s in range(ST)]
    gmoves, mmoves = weight_moves(gate_w, gw, 0), weight_moves(mix_w, mw, 1)
    gfirst, glast, gnear, gline, gon = gmoves
    mfirst, mlast, mnear, mline, mon = mmoves
    for c in (gfirst, fr[0][0], fr[0][1], gnear, mnear):
        c.start()
    along_y(in_sem.at[0])
    pl.semaphore_wait(in_sem.at[0], 3)
    along_z(in_sem.at[1])
    gfirst.wait_recv()
    for c in (*gline, gon[0]):
        c.start()
    gfirst.wait_send()
    glast.start()
    pl.semaphore_wait(in_sem.at[1], 7)

    def gate_part(s, q):
        cols = columns(q)
        pre = jnp.dot(grid[s, my_k, :], gw[q], preferred_element_type=F32)
        mixed = jnp.dot(fv[s], grid[s, :, cols], preferred_element_type=F32)
        gated[s, :, cols] = (mixed * jax.nn.sigmoid(pre)).astype(BF)

    def gate_parts(s, first, last):
        def part(p, _):
            gate_part(s, mp ^ p)
            return 0

        lax.fori_loop(first, last, part, 0)

    def send_whole(s, q, may_be_own):
        def one(u, _):
            to = half_k * TH + partner_half(tm, u)
            src, dst = chan.at[s, q, lax.rem(to, TH)], arrived.at[:, tm, 2 * s + chip]

            def away():
                remote(src, dst, a_send.at[0], a_recv.at[0], (to, q)).start()

            if may_be_own:
                pl.when(to != tm)(away)
                pl.when(to == tm)(lambda: pltpu.make_async_copy(src, dst, a_recv.at[0]).start())
            else:
                away()
            return 0

        lax.fori_loop(0, TH, one, 0, unroll=4)

    def send_half(s, q, h, may_be_own):
        def one(u, _):
            to = half_k * TH + partner_half(tm, u)
            src, dst = chan.at[s, q, lax.rem(to, TH), h], arrived.at[h, tm, 2 * s + chip]

            def away():
                remote(src, dst, a_send.at[1 + h], a_recv.at[1 + h], (to, q)).start()

            if may_be_own:
                pl.when(to != tm)(away)
                pl.when(to == tm)(lambda: pltpu.make_async_copy(src, dst, a_recv.at[1 + h]).start())
            else:
                away()
            return 0

        lax.fori_loop(0, TH, one, 0, unroll=4)

    def mix(s, q):
        v = jnp.dot(gated[s], mw[q], preferred_element_type=F32)
        for h in range(2):
            chan[s, q, :, h] = v[:, h * HALF:(h + 1) * HALF].reshape(TH, LB, HALF).astype(BF)

    def mix_and_send(s, first, last):
        if first == 0:
            mix(s, mp)
            send_whole(s, mp, True)
        def part(p, _):
            mix(s, mp ^ p)
            send_whole(s, mp ^ p, False)
            return 0

        lax.fori_loop(max(first, 1), last, part, 0)

    def mixes_and_halves(s, first):
        if first == 0:
            mix(s, mp)
            send_half(s, mp, 0, True)

        def part(p, _):
            mix(s, mp ^ p)
            send_half(s, mp ^ p, 0, False)
            return 0

        lax.fori_loop(max(first, 1), MP, part, 0)

    def other_halves(s, first):
        if first == 0:
            send_half(s, mp, 1, True)

        def part(p, _):
            send_half(s, mp ^ p, 1, False)
            return 0

        lax.fori_loop(max(first, 1), MP, part, 0)

    def take(s):
        fr[s][0].wait_recv()
        fr[s][2].start()
        if s + 1 < ST:
            fr[s][0].wait_send()
            fr[s + 1][0].start()
            fr[s + 1][1].start()

    def whole(s):
        own[s].wait()
        own[ST + s].wait()
        fr[s][1].wait_recv()
        fr[s][2].wait_recv()

    def gather(last, line, on):
        for n in range(3):
            line[n].wait_recv()
            on[n + 1].start()
        last.wait_recv()
        on[4].start()

    take(0)
    gather(glast, gline, gon)
    glast.wait_send()
    mfirst.start()
    whole(0)
    own[2 * ST].wait()
    gnear.wait_recv()
    gate_parts(0, 0, 2)
    for c in gon:
        c.wait_recv()
    gate_parts(0, 2, MP)
    mfirst.wait_recv()
    for c in (*mline, mon[0]):
        c.start()
    mfirst.wait_send()
    mlast.start()
    own[2 * ST + 1].wait()
    mnear.wait_recv()
    mix_and_send(0, 0, 2)
    take(1)
    whole(1)
    gate_parts(1, 0, MP)
    mix_and_send(1, 0, 2)
    gather(mlast, mline, mon)
    for c in mon:
        c.wait_recv()
    mix_and_send(0, 2, MP)
    take(2)
    mixes_and_halves(1, 2)
    for s in (2, 3):
        if s == 3:
            take(3)
        whole(s)
        gate_parts(s, 0, MP)
        mixes_and_halves(s, 0)
        if s == 2:
            other_halves(1, 2)
    for s in (2, 3):
        other_halves(s, 0)

    own[2 * ST + 2].wait()
    got = arrived.at[:, :, pl.ds(0, 3)]
    pltpu.make_async_copy(got, got, a_recv.at[0]).wait()
    for h in range(2):
        got = arrived.at[h, :, pl.ds(3, 5)]
        pltpu.make_async_copy(got, got, a_recv.at[1 + h]).wait()

        def widen(n, _):
            t = arrived[h, pl.ds(n * 8, 8)]
            rows[pl.ds(pl.multiple_of(n * 512, 512), 512), :] = t.astype(F32).reshape(512, HALF)
            return 0

        lax.fori_loop(0, 8, widen, 0)
        for k in range(LB):
            v = rows[pl.ds(k, NB, stride=LB), :].astype(BF)
            sums[pl.ds(k, NB, stride=LB), :] = jnp.dot(sv[k], v, preferred_element_type=F32)

        def narrow(n, _):
            t = sums[pl.ds(pl.multiple_of(n * 512, 512), 512), :]
            second[h, pl.ds(n * 8, 8)] = t.reshape(8, LB, LB, HALF).astype(BF)
            return 0

        lax.fori_loop(0, 8, narrow, 0)
        half = pl.ds(h * HALF, HALF)
        pltpu.make_async_copy(second.at[h, tm], out.at[:, tm, :, half], o_recv.at[h]).start()

        def place(u, _):
            to = partner(tm, u)
            remote(second.at[h, to], out.at[:, tm, :, half], o_send.at[h], o_recv.at[h], (to, mp)).start()
            return 0

        lax.fori_loop(1, TM, place, 0, unroll=3)

    for s in range(ST):
        fr[s][1].wait_send()
        fr[s][2].wait_send()
    fr[ST - 1][0].wait_send()
    for c in (gnear, *gline, *gon, mnear, mlast, *mline, *mon):
        c.wait_send()

    def left(src, sem):
        pltpu.make_async_copy(src, src, sem).wait()

    keeps = tm // TH == half_k

    def drop_own(part, sem):
        whole, rest = part(TH), part(TH - 1)
        pl.when(keeps)(lambda: left(rest, sem))
        pl.when(jnp.logical_not(keeps))(lambda: left(whole, sem))

    for s, whole_columns in ((0, MP), (1, 2)):
        for q in range(1, whole_columns):
            left(chan.at[s, q], a_send.at[0])
        drop_own(lambda n: chan.at[s, 0, pl.ds(0, n)], a_send.at[0])
    for h in range(2):
        for q in range(2, MP):
            left(chan.at[1, q, :, h], a_send.at[1 + h])
        for s in (2, 3):
            for q in range(1, MP):
                left(chan.at[s, q, :, h], a_send.at[1 + h])
            drop_own(lambda n: chan.at[s, 0, pl.ds(0, n), h], a_send.at[1 + h])
        left(second.at[h, pl.ds(0, TM - 1)], o_send.at[h])
        half = pl.ds(h * HALF, HALF)
        left(out.at[:, :, :, half], o_recv.at[h])


def on_device(frames, first_factor, second_factor, gate_w, mix_w):
    frames = frames.reshape(LB, NB, DW)
    out = pl.pallas_call(
        kernel,
        out_shape=pltpu.VMEM((LB, TM, LB, DW), BF),
        in_specs=[pl.BlockSpec(memory_space=pltpu.HBM)] * 5,
        out_specs=pl.BlockSpec(memory_space=pl.ANY),
        scratch_shapes=[
            pltpu.VMEM((ST, NB, MP * DW), BF),
            pltpu.VMEM((ST, KH, NB), BF),
            pltpu.VMEM((LB, NB, NB), BF),
            pltpu.VMEM((MP, MP * DW, DW), BF),
            pltpu.VMEM((MP, MP * DW, DW), BF),
            pltpu.VMEM((ST, KH, MP * DW), BF),
            pltpu.VMEM((ST, MP, TH, 2, LB, HALF), BF),
            pltpu.VMEM((2, TM, LB, LB, HALF), BF),
            pltpu.VMEM((NB * LB, HALF), F32),
            pltpu.VMEM((NB * LB, HALF), F32),
            pltpu.VMEM((2, TM, LB, LB, HALF), BF),
            pltpu.SemaphoreType.DMA((2 * ST + 3,)),
            pltpu.SemaphoreType.DMA((ST, 3)),
            pltpu.SemaphoreType.DMA((ST, 3)),
            pltpu.SemaphoreType.DMA((2, 11)),
            pltpu.SemaphoreType.DMA((2, 11)),
            pltpu.SemaphoreType.DMA((3,)),
            pltpu.SemaphoreType.DMA((3,)),
            pltpu.SemaphoreType.DMA((2,)),
            pltpu.SemaphoreType.DMA((2,)),
            pltpu.SemaphoreType.REGULAR((2,)),
        ],
        compiler_params=pltpu.CompilerParams(
            collective_id=0, has_side_effects=True, vmem_limit_bytes=56 << 20),
        cost_estimate=pl.CostEstimate(flops=6_500_000_000, bytes_accessed=16 << 20, transcendentals=1 << 20),
        name="monarch",
    )(frames, first_factor, second_factor, gate_w, mix_w)
    return out.reshape(LB * NB, DW)


def solution(mesh):
    in_specs = (
        P("tm", "mp"),
        P("tm", None, None),
        P("tm", None, None),
        P(None, "mp"),
        P(None, "mp"),
    )
    return jax.shard_map(
        on_device, mesh=mesh, in_specs=in_specs, out_specs=P("tm", "mp"), check_vma=False
    )
```
